32 devices in a mesh: sta: 8 (over z, y), tpl: 4 (over x, core).
Axes of the slice: x: 2, y: 2, z: 4, core: 2. Of those that a mesh axis runs over, the one named last changes fastest.
Arguments:
- records: bfloat16 [256, 3, 1024], P(('sta', 'tpl')), may hold values from -180 to 180
- waveforms: bfloat16 [384, 8, 3, 256], P('tpl', 'sta'), may hold values from -54 to 54
- station_ids: int32 [384, 8], P('tpl', 'sta'), may hold values from 0 to 255, as said below
- lag_steps: int32 [384, 8, 3], P('tpl', 'sta'), may hold values from 0 to 255
Outputs:
- network_stack: float32 [384, 512], P('tpl', 'sta')
The draws below stay inside these ranges and needn't reach their ends.
Inputs may be any that keep to these rules, and one draw needn't show every extreme that they name: `station_ids`: stations fall into aligned blocks of 32 (block = station // 32). Within each group of 96 consecutive templates, for every slot, at most 13 templates place that slot in the same block. Slot j of a template lies in block (b + j // 8) mod 8, where b is the block of its slot 0, so at most 13 templates of a group have some slot in one block, a number that some block reaches in every group. The stations of one template are distinct.
All inputs are finite; a program needn't handle non-finite values.
Results may differ from the reference program's by a relative error of at most 0.0003.
Values may be sent and summed in bfloat16 or wider, within the bound.
A program may use at most 64 MiB of HBM per device.

```python
import math
import jax
import jax.numpy as jnp
from jax import lax

STA_DEV = 32
STATIONS = 256
TEMPLATES = 384
TPL_GROUP = 96
TLEN = 256
MAXLAG = 256
WINDOW = 512
SLOTS = 8
CAP = 13
SAMPLES = 1024


def draw_records(key, part):
    key_noise, key_station, key_envelope = jax.random.split(key, 3)
    values = jax.random.truncated_normal(key_noise, -6.0, 6.0, (STATIONS, 3, SAMPLES), jnp.float32)
    station_gain = jnp.exp(jax.random.uniform(key_station, (STATIONS, 3, 1), jnp.float32, 0.0, math.log(3.0)))
    envelope = jnp.exp(jax.random.uniform(key_envelope, (STATIONS, 3, SAMPLES // 64, 1), jnp.float32, 0.0, math.log(10.0)))
    envelope = jnp.broadcast_to(envelope, (STATIONS, 3, SAMPLES // 64, 64)).reshape(STATIONS, 3, SAMPLES)
    return (values * station_gain * envelope).astype(jnp.bfloat16)


def draw_waveforms(key, part):
    key_noise, key_channel, key_piece = jax.random.split(key, 3)
    values = jax.random.truncated_normal(key_noise, -6.0, 6.0, (TEMPLATES, SLOTS, 3, TLEN), jnp.float32)
    channel_gain = jnp.exp(jax.random.uniform(key_channel, (TEMPLATES, SLOTS, 3, 1), jnp.float32, math.log(0.3), math.log(3.0)))
    piece_gain = jnp.exp(jax.random.uniform(key_piece, (TEMPLATES, SLOTS, 3, TLEN // 32, 1), jnp.float32, 0.0, math.log(3.0)))
    piece_gain = jnp.broadcast_to(piece_gain, (TEMPLATES, SLOTS, 3, TLEN // 32, 32)).reshape(TEMPLATES, SLOTS, 3, TLEN)
    return (values * channel_gain * piece_gain).astype(jnp.bfloat16)


def draw_station_ids(key, part):
    subkeys = jax.random.split(key, TEMPLATES // TPL_GROUP)

    def draw_group(group_key):
        key_anchor, key_weight, key_jitter, key_shuffle, key_rotate = jax.random.split(group_key, 5)
        blocks = SLOTS
        extent = SLOTS // 8
        anchor = jax.random.randint(key_anchor, (), 0, blocks)
        weight = jax.random.randint(key_weight, (blocks,), 0, 4)
        jitter = jax.random.randint(key_jitter, (blocks, CAP), 0, 4096)
        offset = (jnp.arange(blocks, dtype=jnp.int32) - anchor) % blocks
        is_hot = offset < extent
        scores = jnp.where(is_hot[:, None], 4 * 4096, weight[:, None] * 4096 + jitter)
        scores = scores * (blocks * CAP) + jnp.arange(blocks * CAP, dtype=jnp.int32).reshape(blocks, CAP)
        chosen = lax.top_k(scores.reshape(-1), TPL_GROUP)[1]
        shuffle = jax.random.permutation(key_shuffle, TPL_GROUP)
        centre = (chosen // CAP)[shuffle]
        rotate = jax.random.randint(key_rotate, (TPL_GROUP,), 0, STA_DEV)
        slot_ids = jnp.arange(SLOTS, dtype=jnp.int32)
        owners = (centre[:, None] + slot_ids[None, :] // 8) % blocks
        within = (rotate[:, None] + slot_ids[None, :] % 8) % STA_DEV
        return (owners * STA_DEV + within).astype(jnp.int32)
    return jax.vmap(draw_group)(subkeys).reshape(TEMPLATES, SLOTS)


def touch_ends(array, stream_key, low, high):
    spot = [jax.random.randint(jax.random.fold_in(stream_key, axis), (), 0, length) for axis, length in enumerate(array.shape)]
    main_axis = array.shape.index(max(array.shape))
    neighbour = spot[:main_axis] + [(spot[main_axis] + 1) % array.shape[main_axis]] + spot[main_axis + 1:]
    return array.at[tuple(spot)].set(low).at[tuple(neighbour)].set(high)


def setup_inputs(seed: int = 0) -> dict:
    key_of = jax.random.split(jax.random.key(seed), 5)
    records = draw_records(jax.random.fold_in(key_of[4], 71), 0)
    waveforms = draw_waveforms(jax.random.fold_in(key_of[4], 71), 0)
    station_ids = draw_station_ids(jax.random.fold_in(key_of[4], 71), 0)
    lag_steps = touch_ends(jax.random.randint(key_of[3], (TEMPLATES, SLOTS, 3), 0, MAXLAG), jax.random.fold_in(key_of[3], 1), 0, MAXLAG - 1).astype(jnp.int32)
    return dict(records=records, waveforms=waveforms, station_ids=station_ids, lag_steps=lag_steps)


epsilon = 1e-05

def window_scale(pieces):
    squares = pieces * pieces
    running = jnp.cumsum(squares, axis=-1)
    running = jnp.concatenate([jnp.zeros(running.shape[:-1] + (1,), running.dtype), running], axis=-1)
    return jnp.sqrt((running[..., TLEN:] - running[..., :-TLEN]) / TLEN + epsilon)

def reference(records, waveforms, station_ids, lag_steps):

    def cut_window(series, offset):
        return lax.dynamic_slice_in_dim(series, offset, WINDOW + TLEN - 1)

    def one_template(block_items):
        wave_rows, stations, offsets = block_items
        station_rows = jnp.take(records, stations.astype(jnp.int32), axis=0)
        pieces = jax.vmap(jax.vmap(cut_window))(station_rows, offsets.astype(jnp.int32)).astype(jnp.float32)
        kernels = wave_rows.astype(jnp.float32)
        transform_size = WINDOW + TLEN
        spectra = jnp.fft.rfft(pieces, n=transform_size, axis=-1) * jnp.conj(jnp.fft.rfft(kernels, n=transform_size, axis=-1))
        raw_terms = jnp.fft.irfft(spectra, n=transform_size, axis=-1)[..., :WINDOW]
        energy_scale = window_scale(pieces)
        template_scale = jnp.sqrt(lax.optimization_barrier(jnp.mean(kernels * kernels, axis=-1)) + epsilon)
        normed = raw_terms / (TLEN * energy_scale * template_scale[..., None])
        return lax.optimization_barrier(jnp.sum(normed, axis=(0, 1)))
    network_stack = lax.map(one_template, (waveforms, station_ids, lag_steps))
    return network_stack.astype(jnp.float32)
```

```python
import functools

import jax
import jax.numpy as jnp
from jax import lax
from jax.experimental import pallas as pl
from jax.experimental.pallas import tpu as pltpu
from jax.sharding import PartitionSpec as P

MAXLAG = 256
WINDOW = 512
LANES = 128
SPLIT = 8
epsilon = 1e-05


def round_up(value, step):
    return (value + step - 1) // step * step


def stack_kernel(
    capacity, padded, details, records, waves, out, wide_records, hankel, scale_rows, wide_waves
):
    channels_all, samples = wide_records.shape
    length = waves.shape[-1] // 3
    taps = length // SPLIT
    width = hankel.shape[-1]
    span = WINDOW + 2 * LANES
    entries = out.shape[0]
    wide_records[...] = records[...].astype(jnp.float32)
    for v in range(wide_waves.shape[0]):
        wide_waves[v] = waves[:, LANES * v : LANES * (v + 1)].astype(jnp.float32)

    def prepare_scales(tile, unused):
        rows = wide_records[pl.ds(pl.multiple_of(tile * 8, 8), 8), :]
        energy = rows * rows
        reach = 1
        while reach < length:
            energy = energy + pltpu.roll(energy, samples - reach, 1)
            reach *= 2
        inverse = lax.rsqrt(energy * (1.0 / length) + epsilon) * (1.0 / length)
        for row in range(SPLIT):
            moved = inverse if row == SPLIT - 1 else pltpu.roll(inverse, SPLIT - 1 - row, 1)
            for v in range(width // LANES):
                scale_rows[v, pl.ds(tile * (8 * SPLIT) + row, 8, stride=SPLIT), :] = moved[
                    :, LANES * v : LANES * (v + 1)
                ]
        return unused

    lax.fori_loop(0, channels_all // 8, prepare_scales, 0)

    def prepare_hankel(channel, unused):
        row = jnp.broadcast_to(wide_records[pl.ds(channel, 1), :], (taps, samples))
        moved = pltpu.roll(
            row, samples - SPLIT * (taps - 1), 1, stride=SPLIT, stride_axis=0
        )
        hankel[channel] = moved[:, :width].astype(jnp.bfloat16)
        return unused

    lax.fori_loop(0, channels_all, prepare_hankel, 0, unroll=2)

    tap = lax.broadcasted_iota(jnp.int32, (length, SPLIT * taps), 0)
    column = lax.broadcasted_iota(jnp.int32, (length, SPLIT * taps), 1)
    spread = jnp.where(tap // SPLIT == taps - 1 - column % taps, 1.0, 0.0).astype(jnp.bfloat16)
    row_id = lax.broadcasted_iota(jnp.int32, (SPLIT * 8, length), 0)
    tap_id = lax.broadcasted_iota(jnp.int32, (SPLIT * 8, length), 1)
    own_phase = tap_id % SPLIT == SPLIT - 1 - row_id % SPLIT
    own_block = tap_id // taps == row_id // SPLIT
    lane = lax.broadcasted_iota(jnp.int32, (SPLIT, LANES), 1)

    def one_entry(entry, unused):
        start = (entry // capacity) * (SPLIT * padded) + entry % capacity
        totals = [jnp.zeros((SPLIT, LANES), jnp.float32) for _ in range(WINDOW // LANES + 1)]
        for channel in range(3):
            parts = length // LANES
            rows = jnp.concatenate(
                [
                    wide_waves[channel * parts + v, pl.ds(start, SPLIT, stride=padded), :]
                    for v in range(parts)
                ],
                axis=1,
            )
            rows = jnp.broadcast_to(rows[:, None, :], (SPLIT, SPLIT, length))
            rows = rows.reshape(SPLIT * SPLIT, length)
            inverse = lax.rsqrt(
                jnp.sum(rows * rows, axis=1, keepdims=True) * (1.0 / length) + epsilon
            )
            phases = jnp.where(own_phase, rows, 0.0).astype(jnp.bfloat16)
            blocks = jnp.dot(phases, spread, preferred_element_type=jnp.float32)
            blocks = jnp.where(own_block, blocks, 0.0).astype(jnp.bfloat16)
            frames = []
            places = []
            for slot in range(SPLIT):
                base = (start + slot * padded) * 4
                place = details[base] * 3 + channel
                lag = details[base + 1 + channel]
                left = pl.multiple_of((lag // LANES) * LANES, LANES)
                places.append((place, lag % LANES, lag // LANES))
                frames.append(hankel[place, :, pl.ds(left, span)])
            terms = jnp.dot(
                blocks, jnp.concatenate(frames, axis=0), preferred_element_type=jnp.float32
            )
            terms = terms * inverse
            for slot in range(SPLIT):
                place, rest, left = places[slot]
                shift = (LANES - rest) % LANES
                scale_at = pl.ds(pl.multiple_of(place * SPLIT, SPLIT), SPLIT)
                moved = []
                for v in range(span // LANES):
                    part = terms[SPLIT * slot : SPLIT * (slot + 1), LANES * v : LANES * (v + 1)]
                    normed = part * scale_rows[left + v, scale_at, :]
                    moved.append(pltpu.roll(normed, shift, 1))
                carried = lane >= LANES - rest
                for v in range(len(totals)):
                    totals[v] = totals[v] + jnp.where(carried, moved[v + 1], moved[v])
        whole = jnp.concatenate(totals, axis=1)
        whole = pltpu.roll(
            whole, whole.shape[1] - (SPLIT - 1), 1, stride=1, stride_axis=0
        )
        out[pl.ds(entry, 1), :] = jnp.sum(whole[:, :WINDOW], axis=0, keepdims=True)
        return unused

    lax.fori_loop(0, entries, one_entry, 0)


def stack_entries(details, records, waves, entries, capacity, padded):
    channels_all, samples = records.shape
    length = waves.shape[-1] // 3
    width = WINDOW + MAXLAG + LANES
    vmem = pl.BlockSpec(memory_space=pltpu.VMEM)
    return pl.pallas_call(
        functools.partial(stack_kernel, capacity, padded),
        out_shape=jax.ShapeDtypeStruct((entries, WINDOW), jnp.float32),
        in_specs=[pl.BlockSpec(memory_space=pltpu.SMEM), vmem, vmem],
        out_specs=vmem,
        scratch_shapes=[
            pltpu.VMEM((channels_all, samples), jnp.float32),
            pltpu.VMEM((channels_all, length // SPLIT, width), jnp.bfloat16),
            pltpu.VMEM((width // LANES, channels_all * SPLIT, LANES), jnp.float32),
            pltpu.VMEM((waves.shape[1] // LANES, waves.shape[0], LANES), jnp.float32),
        ],
        compiler_params=pltpu.CompilerParams(vmem_limit_bytes=40 * 1024 * 1024),
        name="stack_entries",
    )(details, records, waves)


def on_device(records, waveforms, station_ids, lag_steps):
    owners = lax.axis_size("sta")
    groups = waveforms.shape[0]
    length = waveforms.shape[-1]
    block_stations = records.shape[0] * lax.axis_size("tpl")
    spread = owners // SPLIT
    capacity = (groups + owners - 1) // owners + 1
    padded = round_up(capacity, 16)
    stations = station_ids[:, 0]
    owner = stations // block_stations
    earlier = jnp.arange(groups)[None, :] < jnp.arange(groups)[:, None]
    rank = jnp.sum((owner[:, None] == owner[None, :]) & earlier, axis=1, dtype=jnp.int32)

    details = jnp.concatenate([(stations % block_stations)[:, None], lag_steps[:, 0, :]], axis=1)
    payload = jnp.concatenate(
        [
            waveforms.reshape(groups, 3 * length),
            jnp.pad(details.astype(jnp.bfloat16), ((0, 0), (0, LANES - 4))),
        ],
        axis=1,
    )
    place = owner * padded + rank
    select = (jnp.arange(owners * padded)[:, None] == place[None, :]).astype(jnp.bfloat16)
    send = jnp.dot(select, payload, preferred_element_type=jnp.float32).astype(jnp.bfloat16)
    got = lax.all_to_all(send, "sta", split_axis=0, concat_axis=0, tiled=True)
    gathered = lax.all_gather(
        records.reshape(-1, records.shape[-1]), "tpl", axis=0, tiled=True
    )
    got_details = got[:, 3 * length : 3 * length + 4].astype(jnp.int32).reshape(-1)
    entries = spread * capacity
    stacks = stack_entries(
        got_details, gathered, got[:, : 3 * length], entries, capacity, padded
    )
    piece = WINDOW // owners
    pieces = stacks.reshape(entries, owners, piece).transpose(1, 0, 2)
    pieces = lax.all_to_all(pieces, "sta", split_axis=0, concat_axis=0, tiled=True)
    pieces = pieces.reshape(owners * entries, piece)
    first = (owner - lax.axis_index("sta") // SPLIT) % owners
    steps = jnp.arange(spread)[None, :]
    wanted = ((first[:, None] + steps) % owners * spread + steps) * capacity + rank[:, None]
    marks = jnp.sum(
        wanted[:, :, None] == jnp.arange(owners * entries)[None, None, :], axis=1
    ).astype(jnp.float32)
    return jnp.dot(
        marks, pieces, precision=lax.Precision.HIGHEST, preferred_element_type=jnp.float32
    )


def solution(mesh):
    in_specs = (
        P(("sta", "tpl"), None, None),
        P("tpl", "sta", None, None),
        P("tpl", "sta"),
        P("tpl", "sta", None),
    )
    out_specs = P("tpl", "sta")
    return jax.shard_map(
        on_device, mesh=mesh, in_specs=in_specs, out_specs=out_specs, check_vma=False
    )
```

```python
import functools

import jax
import jax.numpy as jnp
from jax import lax
from jax.experimental import pallas as pl
from jax.experimental.pallas import tpu as pltpu
from jax.sharding import PartitionSpec as P

MAXLAG = 256
WINDOW = 512
LANES = 128
SPLIT = 8
epsilon = 1e-05
MESH = pl.DeviceIdType.MESH


def round_up(value, step):
    return (value + step - 1) // step * step


def exchange_kernel(sizes, send, records, got, gathered, keep_sems, send_sems, recv_sems):
    owners, sharers, padded = sizes
    me = lax.axis_index("sta")
    part = lax.axis_index("tpl")
    others = [lax.rem(me + step, owners) for step in range(1, owners)]
    sharing = [lax.rem(part + step, sharers) for step in range(1, sharers)]
    barrier = pltpu.get_barrier_semaphore()
    for other in others:
        pl.semaphore_signal(barrier, inc=1, device_id={"sta": other}, device_id_type=MESH)
    for other in sharing:
        pl.semaphore_signal(barrier, inc=1, device_id={"tpl": other}, device_id_type=MESH)
    own = pl.ds(pl.multiple_of(me * padded, padded), padded)
    kept = [
        pltpu.make_async_copy(send.at[own], got.at[own], keep_sems.at[0]),
        pltpu.make_async_copy(records, gathered.at[part], keep_sems.at[1]),
    ]
    for copy in kept:
        copy.start()
    pl.semaphore_wait(barrier, len(others) + len(sharing))
    copies = []
    for other in sharing:
        copies.append((records, gathered.at[part], {"tpl": other}))
    for other in others:
        rows = pl.ds(pl.multiple_of(other * padded, padded), padded)
        copies.append((send.at[rows], got.at[own], {"sta": other}))
    copies = [
        pltpu.make_async_remote_copy(
            src_ref=source,
            dst_ref=target,
            send_sem=send_sems.at[index],
            recv_sem=recv_sems.at[index],
            device_id=device,
            device_id_type=MESH,
        )
        for index, (source, target, device) in enumerate(copies)
    ]
    for copy in copies:
        copy.start()
    for copy in kept + copies:
        copy.wait()


def exchange(send, records, owners, sharers):
    count = owners + sharers - 2
    anywhere = pl.BlockSpec(memory_space=pl.ANY)
    return pl.pallas_call(
        functools.partial(exchange_kernel, (owners, sharers, send.shape[0] // owners)),
        out_shape=(
            jax.ShapeDtypeStruct(send.shape, send.dtype),
            jax.ShapeDtypeStruct((sharers,) + records.shape, records.dtype),
        ),
        in_specs=[anywhere, anywhere],
        out_specs=(anywhere, anywhere),
        scratch_shapes=[
            pltpu.SemaphoreType.DMA((2,)),
            pltpu.SemaphoreType.DMA((count,)),
            pltpu.SemaphoreType.DMA((count,)),
        ],
        compiler_params=pltpu.CompilerParams(collective_id=0, has_side_effects=True),
        name="exchange",
    )(send, records)


def deliver_kernel(owners, stacks, wanted, out, got, send_sems, recv_sems):
    me = lax.axis_index("sta")
    piece = WINDOW // owners
    entries = stacks.shape[0]
    others = [lax.rem(me + step, owners) for step in range(1, owners)]
    barrier = pltpu.get_barrier_semaphore()
    for other in others:
        pl.semaphore_signal(barrier, inc=1, device_id={"sta": other}, device_id_type=MESH)

    def columns(device):
        start = (device * piece) // LANES * LANES
        return pl.ds(pl.multiple_of(start, LANES), LANES)

    own = pl.ds(pl.multiple_of(me * entries, 8), entries)
    got[own, :] = stacks[:, columns(me)]
    pl.semaphore_wait(barrier, len(others))
    copies = [
        pltpu.make_async_remote_copy(
            src_ref=stacks.at[:, columns(other)],
            dst_ref=got.at[own],
            send_sem=send_sems.at[index],
            recv_sem=recv_sems.at[index],
            device_id={"sta": other},
            device_id_type=MESH,
        )
        for index, other in enumerate(others)
    ]
    for copy in copies:
        copy.start()
    places = lax.broadcasted_iota(jnp.int32, (wanted.shape[0], got.shape[0]), 1)
    marks = jnp.zeros(places.shape, jnp.float32)
    for step in range(wanted.shape[1]):
        marks = marks + jnp.where(wanted[:, step : step + 1] == places, 1.0, 0.0)
    for copy in copies:
        copy.wait()
    out[...] = jnp.dot(
        marks, got[...], precision=lax.Precision.HIGHEST, preferred_element_type=jnp.float32
    )


def deliver(stacks, wanted, owners):
    vmem = pl.BlockSpec(memory_space=pltpu.VMEM)
    return pl.pallas_call(
        functools.partial(deliver_kernel, owners),
        out_shape=jax.ShapeDtypeStruct((wanted.shape[0], LANES), jnp.float32),
        in_specs=[vmem, vmem],
        out_specs=vmem,
        scratch_shapes=[
            pltpu.VMEM((owners * stacks.shape[0], LANES), jnp.float32),
            pltpu.SemaphoreType.DMA((owners - 1,)),
            pltpu.SemaphoreType.DMA((owners - 1,)),
        ],
        compiler_params=pltpu.CompilerParams(
            collective_id=1, has_side_effects=True, vmem_limit_bytes=32 * 1024 * 1024
        ),
        name="deliver",
    )(stacks, wanted)


def stack_kernel(
    sizes,
    details,
    records,
    waves,
    out,
    wide_records,
    hankel,
    scale_rows,
    wide_waves,
    wave_blocks,
    wave_scales,
):
    entries, capacity, padded, length = sizes
    channels_all, samples = wide_records.shape
    sharers = records.shape[0]
    rows_each = channels_all // sharers
    taps = length // SPLIT
    width = hankel.shape[-1]
    span = WINDOW + 2 * LANES
    parts = length // LANES
    for sharer in range(sharers):
        wide_records[rows_each * sharer : rows_each * (sharer + 1)] = records[
            sharer, :rows_each
        ].astype(jnp.float32)
    for v in range(wide_waves.shape[0]):
        wide_waves[v] = waves[:, LANES * v : LANES * (v + 1)].astype(jnp.float32)

    tap = lax.broadcasted_iota(jnp.int32, (length, SPLIT * taps), 0)
    column = lax.broadcasted_iota(jnp.int32, (length, SPLIT * taps), 1)
    spread = jnp.where(tap // SPLIT == taps - 1 - column % taps, 1.0, 0.0).astype(jnp.bfloat16)
    row_id = lax.broadcasted_iota(jnp.int32, (SPLIT * 8, length), 0)
    tap_id = lax.broadcasted_iota(jnp.int32, (SPLIT * 8, length), 1)
    own_phase = tap_id % SPLIT == SPLIT - 1 - row_id % SPLIT
    own_block = tap_id // taps == row_id // SPLIT

    def first_row(entry):
        return (entry // capacity) * (SPLIT * padded) + entry % capacity

    def prepare_waves(entry, unused):
        start = first_row(entry)
        phases = []
        for channel in range(3):
            rows = jnp.concatenate(
                [
                    wide_waves[channel * parts + v, pl.ds(start, SPLIT, stride=padded), :]
                    for v in range(parts)
                ],
                axis=1,
            )
            inverse = lax.rsqrt(
                jnp.sum(rows * rows, axis=1, keepdims=True) * (1.0 / length) + epsilon
            )
            inverse = jnp.broadcast_to(inverse[:, None, :], (SPLIT, SPLIT, LANES))
            wave_scales[entry, channel] = inverse
            rows = jnp.broadcast_to(rows[:, None, :], (SPLIT, SPLIT, length))
            rows = rows.reshape(SPLIT * SPLIT, length)
            phases.append(jnp.where(own_phase, rows, 0.0).astype(jnp.bfloat16))
        blocks = jnp.dot(
            jnp.concatenate(phases, axis=0), spread, preferred_element_type=jnp.float32
        )
        for channel in range(3):
            block = blocks[SPLIT * SPLIT * channel : SPLIT * SPLIT * (channel + 1)]
            wave_blocks[entry, channel] = jnp.where(own_block, block, 0.0).astype(jnp.bfloat16)
        return unused

    lax.fori_loop(0, entries, prepare_waves, 0, unroll=True)

    tile_rows = 32

    def prepare_scales(tile, unused):
        rows = wide_records[pl.ds(pl.multiple_of(tile * tile_rows, tile_rows), tile_rows), :]
        energy = rows * rows
        reach = 1
        while reach < length:
            energy = energy + pltpu.roll(energy, samples - reach, 1)
            reach *= 2
        inverse = lax.rsqrt(energy * (1.0 / length) + epsilon) * (1.0 / length)
        for row in range(SPLIT):
            moved = inverse if row == SPLIT - 1 else pltpu.roll(inverse, SPLIT - 1 - row, 1)
            for v in range(width // LANES):
                for eight in range(tile_rows // 8):
                    at = (tile * tile_rows + 8 * eight) * SPLIT + row
                    scale_rows[v, pl.ds(at, 8, stride=SPLIT), :] = moved[
                        8 * eight : 8 * (eight + 1), LANES * v : LANES * (v + 1)
                    ]
        return unused

    lax.fori_loop(0, channels_all // tile_rows, prepare_scales, 0)

    def prepare_hankel(channel, unused):
        row = jnp.broadcast_to(wide_records[pl.ds(channel, 1), :], (taps, samples))
        moved = pltpu.roll(
            row, samples - SPLIT * (taps - 1), 1, stride=SPLIT, stride_axis=0
        )
        hankel[channel] = moved[:, :width].astype(jnp.bfloat16)
        return unused

    lax.fori_loop(0, channels_all, prepare_hankel, 0, unroll=8)

    lane = lax.broadcasted_iota(jnp.int32, (SPLIT, LANES), 1)
    out[...] = jnp.zeros_like(out)

    def one_entry(entry):
        start = first_row(entry)
        totals = [jnp.zeros((SPLIT, LANES), jnp.float32) for _ in range(WINDOW // LANES + 1)]
        for channel in range(3):
            frames = []
            places = []
            for slot in range(SPLIT):
                base = (start + slot * padded) * 4
                place = details[base] * 3 + channel
                lag = details[base + 1 + channel]
                left = pl.multiple_of((lag // LANES) * LANES, LANES)
                places.append((place, lag % LANES, lag // LANES))
                frames.append(hankel[place, :, pl.ds(left, span)])
            terms = jnp.dot(
                wave_blocks[entry, channel],
                jnp.concatenate(frames, axis=0),
                preferred_element_type=jnp.float32,
            )
            for slot in range(SPLIT):
                place, rest, left = places[slot]
                shift = (LANES - rest) % LANES
                scale_at = pl.ds(pl.multiple_of(place * SPLIT, SPLIT), SPLIT)
                inverse = wave_scales[entry, channel, slot]
                moved = []
                for v in range(span // LANES):
                    part = terms[SPLIT * slot : SPLIT * (slot + 1), LANES * v : LANES * (v + 1)]
                    normed = part * (scale_rows[left + v, scale_at, :] * inverse)
                    moved.append(pltpu.roll(normed, shift, 1))
                carried = lane >= LANES - rest
                for v in range(len(totals)):
                    totals[v] = totals[v] + jnp.where(carried, moved[v + 1], moved[v])
        whole = jnp.concatenate(totals, axis=1)
        whole = pltpu.roll(
            whole, whole.shape[1] - (SPLIT - 1), 1, stride=1, stride_axis=0
        )
        out[pl.ds(entry, 1), :] = jnp.sum(whole[:, :WINDOW], axis=0, keepdims=True)

    def some_entries(turn, unused):
        for step in range(2):
            one_entry(jnp.minimum(turn * 2 + step, entries - 1))
        return unused

    lax.fori_loop(0, (entries + 1) // 2, some_entries, 0)


def stack_entries(details, records, waves, rows_each, length, entries, capacity, padded):
    sharers, _, samples = records.shape
    channels_all = sharers * rows_each
    width = WINDOW + MAXLAG + LANES
    vmem = pl.BlockSpec(memory_space=pltpu.VMEM)
    return pl.pallas_call(
        functools.partial(stack_kernel, (entries, capacity, padded, length)),
        out_shape=jax.ShapeDtypeStruct((round_up(entries, 8), WINDOW), jnp.float32),
        in_specs=[pl.BlockSpec(memory_space=pltpu.SMEM), vmem, vmem],
        out_specs=vmem,
        scratch_shapes=[
            pltpu.VMEM((channels_all, samples), jnp.float32),
            pltpu.VMEM((channels_all, length // SPLIT, width), jnp.bfloat16),
            pltpu.VMEM((width // LANES, channels_all * SPLIT, LANES), jnp.float32),
            pltpu.VMEM((3 * length // LANES, waves.shape[0], LANES), jnp.float32),
            pltpu.VMEM((entries, 3, SPLIT * SPLIT, length), jnp.bfloat16),
            pltpu.VMEM((entries, 3, SPLIT, SPLIT, LANES), jnp.float32),
        ],
        compiler_params=pltpu.CompilerParams(vmem_limit_bytes=40 * 1024 * 1024),
        name="stack_entries",
    )(details, records, waves)


def on_device(records, waveforms, station_ids, lag_steps):
    owners = lax.axis_size("sta")
    sharers = lax.axis_size("tpl")
    groups = waveforms.shape[0]
    length = waveforms.shape[-1]
    block_stations = records.shape[0] * sharers
    spread = owners // SPLIT
    capacity = (groups + owners - 1) // owners + 1
    padded = round_up(capacity, 16)
    stations = station_ids[:, 0]
    owner = stations // block_stations
    earlier = jnp.arange(groups)[None, :] < jnp.arange(groups)[:, None]
    rank = jnp.sum((owner[:, None] == owner[None, :]) & earlier, axis=1, dtype=jnp.int32)

    details = jnp.concatenate([(stations % block_stations)[:, None], lag_steps[:, 0, :]], axis=1)
    payload = jnp.concatenate(
        [
            waveforms.reshape(groups, 3 * length),
            jnp.pad(details.astype(jnp.bfloat16), ((0, 0), (0, LANES - 4))),
        ],
        axis=1,
    )
    place = owner * padded + rank
    select = (jnp.arange(owners * padded)[:, None] == place[None, :]).astype(jnp.bfloat16)
    send = jnp.dot(select, payload, preferred_element_type=jnp.float32).astype(jnp.bfloat16)
    rows_each = records.shape[0] * 3
    flat_records = records.reshape(rows_each, records.shape[-1])
    flat_records = jnp.pad(flat_records, ((0, round_up(rows_each, 16) - rows_each), (0, 0)))
    got, gathered = exchange(send, flat_records, owners, sharers)
    got_details = got[:, 3 * length : 3 * length + 4].astype(jnp.int32).reshape(-1)
    entries = spread * capacity
    stacks = stack_entries(
        got_details, gathered, got, rows_each, length, entries, capacity, padded
    )
    first = (owner - lax.axis_index("sta") // SPLIT) % owners
    steps = jnp.arange(spread)[None, :]
    wanted = (first[:, None] + steps) % owners * stacks.shape[0] + steps * capacity
    wanted = wanted + rank[:, None]
    piece = WINDOW // owners
    rows = deliver(stacks, wanted, owners)
    return lax.dynamic_slice_in_dim(rows, lax.axis_index("sta") * piece % LANES, piece, 1)


def solution(mesh):
    in_specs = (
        P(("sta", "tpl"), None, None),
        P("tpl", "sta", None, None),
        P("tpl", "sta"),
        P("tpl", "sta", None),
    )
    out_specs = P("tpl", "sta")
    return jax.shard_map(
        on_device, mesh=mesh, in_specs=in_specs, out_specs=out_specs, check_vma=False
    )
```

```python
import functools

import jax
import jax.numpy as jnp
from jax import lax
from jax.experimental import pallas as pl
from jax.experimental.pallas import tpu as pltpu
from jax.sharding import PartitionSpec as P

MAXLAG = 256
WINDOW = 512
LANES = 128
SPLIT = 8
epsilon = 1e-05
MESH = pl.DeviceIdType.MESH


def round_up(value, step):
    return (value + step - 1) // step * step


def exchange_kernel(
    sizes,
    waves,
    stations,
    lags,
    records,
    got,
    gathered,
    wanted,
    send,
    keep_sems,
    send_sems,
    recv_sems,
):
    owners, sharers, padded, capacity, block_stations, stack_rows = sizes
    groups, wave_width = waves.shape
    me = lax.axis_index("sta")
    part = lax.axis_index("tpl")
    others = [lax.rem(me + step, owners) for step in range(1, owners)]
    sharing = [lax.rem(part + step, sharers) for step in range(1, sharers)]
    barrier = pltpu.get_barrier_semaphore()
    for other in others:
        pl.semaphore_signal(barrier, inc=1, device_id={"sta": other}, device_id_type=MESH)
    for other in sharing:
        pl.semaphore_signal(barrier, inc=1, device_id={"tpl": other}, device_id_type=MESH)
    own = pl.ds(pl.multiple_of(me * padded, padded), padded)

    def remote(index, source, target, device):
        return pltpu.make_async_remote_copy(
            src_ref=source,
            dst_ref=target,
            send_sem=send_sems.at[index],
            recv_sem=recv_sems.at[index],
            device_id=device,
            device_id_type=MESH,
        )

    owner = stations[...] // block_stations
    block_id = lax.broadcasted_iota(jnp.int32, (groups, LANES), 1)
    member = jnp.where(owner == block_id, 1.0, 0.0)
    row = lax.broadcasted_iota(jnp.int32, (groups, groups), 0)
    earlier = row > lax.broadcasted_iota(jnp.int32, (groups, groups), 1)
    before = jnp.dot(
        jnp.where(earlier, 1.0, 0.0).astype(jnp.bfloat16),
        member.astype(jnp.bfloat16),
        preferred_element_type=jnp.float32,
    )
    rank = jnp.sum(before * member, axis=1, keepdims=True).astype(jnp.int32)
    places = lax.broadcasted_iota(jnp.int32, (groups, owners * padded), 1)
    select = jnp.where(owner * padded + rank == places, 1.0, 0.0).astype(jnp.bfloat16)
    first = owner - me // SPLIT
    block = jnp.where(first < 0, first + owners, first) + block_id
    block = jnp.where(block >= owners, block - owners, block)
    wanted[...] = block * stack_rows + block_id * capacity + rank
    detail = stations[...] - owner * block_stations
    for channel in range(3):
        detail = jnp.where(block_id == channel + 1, lags[:, channel : channel + 1], detail)
    detail = detail.astype(jnp.float32).astype(jnp.bfloat16)
    for start, rows in ((0, waves[...]), (wave_width, detail)):
        send[:, start : start + rows.shape[1]] = lax.dot_general(
            select, rows, (((0,), (0,)), ((), ())), preferred_element_type=jnp.float32
        ).astype(jnp.bfloat16)

    kept = [
        pltpu.make_async_copy(send.at[own], got.at[own], keep_sems.at[0]),
        pltpu.make_async_copy(records, gathered.at[part], keep_sems.at[1]),
    ]
    copies = []
    for other in others:
        rows = pl.ds(pl.multiple_of(other * padded, padded), padded)
        copies.append(remote(len(copies), send.at[rows], got.at[own], {"sta": other}))
    for other in sharing:
        copies.append(remote(len(copies), records, gathered.at[part], {"tpl": other}))
    pl.semaphore_wait(barrier, len(others) + len(sharing))
    for copy in copies + kept:
        copy.start()
    for copy in copies + kept:
        copy.wait()


def exchange(waves, stations, lags, records, sizes):
    owners, sharers, padded = sizes[:3]
    count = owners + sharers - 2
    anywhere = pl.BlockSpec(memory_space=pl.ANY)
    vmem = pl.BlockSpec(memory_space=pltpu.VMEM)
    sent = (owners * padded, waves.shape[1] + LANES)
    return pl.pallas_call(
        functools.partial(exchange_kernel, sizes),
        out_shape=(
            jax.ShapeDtypeStruct(sent, waves.dtype),
            jax.ShapeDtypeStruct((sharers,) + records.shape, records.dtype),
            jax.ShapeDtypeStruct((waves.shape[0], LANES), jnp.int32),
        ),
        in_specs=[vmem, vmem, vmem, vmem],
        out_specs=(anywhere, anywhere, vmem),
        scratch_shapes=[
            pltpu.VMEM(sent, waves.dtype),
            pltpu.SemaphoreType.DMA((2,)),
            pltpu.SemaphoreType.DMA((count,)),
            pltpu.SemaphoreType.DMA((count,)),
        ],
        compiler_params=pltpu.CompilerParams(
            collective_id=0, has_side_effects=True, vmem_limit_bytes=32 * 1024 * 1024
        ),
        name="exchange",
    )(waves, stations, lags, records)


def deliver_kernel(owners, spread, stacks, wanted, out, got, send_sems, recv_sems):
    me = lax.axis_index("sta")
    piece = WINDOW // owners
    entries = stacks.shape[0]
    others = [lax.rem(me + step, owners) for step in range(1, owners)]
    barrier = pltpu.get_barrier_semaphore()
    for other in others:
        pl.semaphore_signal(barrier, inc=1, device_id={"sta": other}, device_id_type=MESH)

    def columns(device):
        start = (device * piece) // LANES * LANES
        return pl.ds(pl.multiple_of(start, LANES), LANES)

    own = pl.ds(pl.multiple_of(me * entries, 8), entries)
    got[own, :] = stacks[:, columns(me)]
    pl.semaphore_wait(barrier, len(others))
    copies = [
        pltpu.make_async_remote_copy(
            src_ref=stacks.at[:, columns(other)],
            dst_ref=got.at[own],
            send_sem=send_sems.at[index],
            recv_sem=recv_sems.at[index],
            device_id={"sta": other},
            device_id_type=MESH,
        )
        for index, other in enumerate(others)
    ]
    for copy in copies:
        copy.start()
    places = lax.broadcasted_iota(jnp.int32, (wanted.shape[0], got.shape[0]), 1)
    marks = jnp.zeros(places.shape, jnp.float32)
    for step in range(spread):
        marks = marks + jnp.where(wanted[:, step : step + 1] == places, 1.0, 0.0)
    for copy in copies:
        copy.wait()
    out[...] = jnp.dot(
        marks, got[...], precision=lax.Precision.HIGHEST, preferred_element_type=jnp.float32
    )


def deliver(stacks, wanted, owners, spread):
    vmem = pl.BlockSpec(memory_space=pltpu.VMEM)
    return pl.pallas_call(
        functools.partial(deliver_kernel, owners, spread),
        out_shape=jax.ShapeDtypeStruct((wanted.shape[0], LANES), jnp.float32),
        in_specs=[vmem, vmem],
        out_specs=vmem,
        scratch_shapes=[
            pltpu.VMEM((owners * stacks.shape[0], LANES), jnp.float32),
            pltpu.SemaphoreType.DMA((owners - 1,)),
            pltpu.SemaphoreType.DMA((owners - 1,)),
        ],
        compiler_params=pltpu.CompilerParams(
            collective_id=1, has_side_effects=True, vmem_limit_bytes=32 * 1024 * 1024
        ),
        name="deliver",
    )(stacks, wanted)


def stack_kernel(
    sizes,
    details,
    records,
    waves,
    out,
    wide_records,
    hankel,
    scale_rows,
    wide_waves,
    wave_blocks,
    wave_scales,
):
    entries, capacity, padded, length = sizes
    channels_all, samples = wide_records.shape
    sharers = records.shape[0]
    rows_each = channels_all // sharers
    taps = length // SPLIT
    width = hankel.shape[-1]
    span = WINDOW + 2 * LANES
    parts = length // LANES
    for sharer in range(sharers):
        wide_records[rows_each * sharer : rows_each * (sharer + 1)] = records[
            sharer, :rows_each
        ].astype(jnp.float32)
    for v in range(wide_waves.shape[0]):
        wide_waves[v] = waves[:, LANES * v : LANES * (v + 1)].astype(jnp.float32)

    tap = lax.broadcasted_iota(jnp.int32, (length, SPLIT * taps), 0)
    column = lax.broadcasted_iota(jnp.int32, (length, SPLIT * taps), 1)
    spread = jnp.where(tap // SPLIT == taps - 1 - column % taps, 1.0, 0.0).astype(jnp.bfloat16)
    row_id = lax.broadcasted_iota(jnp.int32, (SPLIT * 8, length), 0)
    tap_id = lax.broadcasted_iota(jnp.int32, (SPLIT * 8, length), 1)
    own_phase = tap_id % SPLIT == SPLIT - 1 - row_id % SPLIT
    own_block = tap_id // taps == row_id // SPLIT

    def first_row(entry):
        return (entry // capacity) * (SPLIT * padded) + entry % capacity

    def prepare_waves(entry, unused):
        start = first_row(entry)
        phases = []
        for channel in range(3):
            rows = jnp.concatenate(
                [
                    wide_waves[channel * parts + v, pl.ds(start, SPLIT, stride=padded), :]
                    for v in range(parts)
                ],
                axis=1,
            )
            inverse = lax.rsqrt(
                jnp.sum(rows * rows, axis=1, keepdims=True) * (1.0 / length) + epsilon
            )
            inverse = jnp.broadcast_to(inverse[:, None, :], (SPLIT, SPLIT, LANES))
            wave_scales[entry, channel] = inverse
            rows = jnp.broadcast_to(rows[:, None, :], (SPLIT, SPLIT, length))
            rows = rows.reshape(SPLIT * SPLIT, length)
            phases.append(jnp.where(own_phase, rows, 0.0).astype(jnp.bfloat16))
        blocks = jnp.dot(
            jnp.concatenate(phases, axis=0), spread, preferred_element_type=jnp.float32
        )
        for channel in range(3):
            block = blocks[SPLIT * SPLIT * channel : SPLIT * SPLIT * (channel + 1)]
            wave_blocks[entry, channel] = jnp.where(own_block, block, 0.0).astype(jnp.bfloat16)
        return unused

    lax.fori_loop(0, entries, prepare_waves, 0, unroll=True)

    tile_rows = 32

    def prepare_scales(tile, unused):
        rows = wide_records[pl.ds(pl.multiple_of(tile * tile_rows, tile_rows), tile_rows), :]
        energy = rows * rows
        reach = 1
        while reach < length:
            energy = energy + pltpu.roll(energy, samples - reach, 1)
            reach *= 2
        inverse = lax.rsqrt(energy * (1.0 / length) + epsilon) * (1.0 / length)
        for row in range(SPLIT):
            moved = inverse if row == SPLIT - 1 else pltpu.roll(inverse, SPLIT - 1 - row, 1)
            for v in range(width // LANES):
                for eight in range(tile_rows // 8):
                    at = (tile * tile_rows + 8 * eight) * SPLIT + row
                    scale_rows[v, pl.ds(at, 8, stride=SPLIT), :] = moved[
                        8 * eight : 8 * (eight + 1), LANES * v : LANES * (v + 1)
                    ]
        return unused

    lax.fori_loop(0, channels_all // tile_rows, prepare_scales, 0)

    def prepare_hankel(channel, unused):
        row = jnp.broadcast_to(wide_records[pl.ds(channel, 1), :], (taps, samples))
        moved = pltpu.roll(
            row, samples - SPLIT * (taps - 1), 1, stride=SPLIT, stride_axis=0
        )
        hankel[channel] = moved[:, :width].astype(jnp.bfloat16)
        return unused

    lax.fori_loop(0, channels_all, prepare_hankel, 0, unroll=8)

    lane = lax.broadcasted_iota(jnp.int32, (SPLIT, LANES), 1)
    out[...] = jnp.zeros_like(out)

    def one_entry(entry):
        start = first_row(entry)
        totals = [jnp.zeros((SPLIT, LANES), jnp.float32) for _ in range(WINDOW // LANES + 1)]
        for channel in range(3):
            frames = []
            places = []
            for slot in range(SPLIT):
                base = (start + slot * padded) * 4
                place = details[base] * 3 + channel
                lag = details[base + 1 + channel]
                left = pl.multiple_of((lag // LANES) * LANES, LANES)
                places.append((place, lag % LANES, lag // LANES))
                frames.append(hankel[place, :, pl.ds(left, span)])
            terms = jnp.dot(
                wave_blocks[entry, channel],
                jnp.concatenate(frames, axis=0),
                preferred_element_type=jnp.float32,
            )
            for slot in range(SPLIT):
                place, rest, left = places[slot]
                shift = (LANES - rest) % LANES
                scale_at = pl.ds(pl.multiple_of(place * SPLIT, SPLIT), SPLIT)
                inverse = wave_scales[entry, channel, slot]
                moved = []
                for v in range(span // LANES):
                    part = terms[SPLIT * slot : SPLIT * (slot + 1), LANES * v : LANES * (v + 1)]
                    normed = part * (scale_rows[left + v, scale_at, :] * inverse)
                    moved.append(pltpu.roll(normed, shift, 1))
                carried = lane >= LANES - rest
                for v in range(len(totals)):
                    totals[v] = totals[v] + jnp.where(carried, moved[v + 1], moved[v])
        whole = jnp.concatenate(totals, axis=1)
        whole = pltpu.roll(
            whole, whole.shape[1] - (SPLIT - 1), 1, stride=1, stride_axis=0
        )
        out[pl.ds(entry, 1), :] = jnp.sum(whole[:, :WINDOW], axis=0, keepdims=True)

    def some_entries(turn, unused):
        for step in range(2):
            one_entry(jnp.minimum(turn * 2 + step, entries - 1))
        return unused

    lax.fori_loop(0, (entries + 1) // 2, some_entries, 0)


def stack_entries(details, records, waves, rows_each, length, entries, capacity, padded):
    sharers, _, samples = records.shape
    channels_all = sharers * rows_each
    width = WINDOW + MAXLAG + LANES
    vmem = pl.BlockSpec(memory_space=pltpu.VMEM)
    return pl.pallas_call(
        functools.partial(stack_kernel, (entries, capacity, padded, length)),
        out_shape=jax.ShapeDtypeStruct((round_up(entries, 8), WINDOW), jnp.float32),
        in_specs=[pl.BlockSpec(memory_space=pltpu.SMEM), vmem, vmem],
        out_specs=vmem,
        scratch_shapes=[
            pltpu.VMEM((channels_all, samples), jnp.float32),
            pltpu.VMEM((channels_all, length // SPLIT, width), jnp.bfloat16),
            pltpu.VMEM((width // LANES, channels_all * SPLIT, LANES), jnp.float32),
            pltpu.VMEM((3 * length // LANES, waves.shape[0], LANES), jnp.float32),
            pltpu.VMEM((entries, 3, SPLIT * SPLIT, length), jnp.bfloat16),
            pltpu.VMEM((entries, 3, SPLIT, SPLIT, LANES), jnp.float32),
        ],
        compiler_params=pltpu.CompilerParams(vmem_limit_bytes=40 * 1024 * 1024),
        name="stack_entries",
    )(details, records, waves)


def on_device(records, waveforms, station_ids, lag_steps):
    owners = lax.axis_size("sta")
    sharers = lax.axis_size("tpl")
    groups = waveforms.shape[0]
    length = waveforms.shape[-1]
    block_stations = records.shape[0] * sharers
    spread = owners // SPLIT
    capacity = (groups + owners - 1) // owners + 1
    padded = round_up(capacity, 16)
    rows_each = records.shape[0] * 3
    flat_records = records.reshape(rows_each, records.shape[-1])
    flat_records = jnp.pad(flat_records, ((0, round_up(rows_each, 16) - rows_each), (0, 0)))
    entries = spread * capacity
    stack_rows = round_up(entries, 8)
    got, gathered, wanted = exchange(
        waveforms.reshape(groups, 3 * length),
        station_ids,
        lag_steps[:, 0, :],
        flat_records,
        (owners, sharers, padded, capacity, block_stations, stack_rows),
    )
    got_details = got[:, 3 * length : 3 * length + 4].astype(jnp.int32).reshape(-1)
    stacks = stack_entries(
        got_details, gathered, got, rows_each, length, entries, capacity, padded
    )
    rows = deliver(stacks, wanted, owners, spread)
    piece = WINDOW // owners
    return lax.dynamic_slice_in_dim(rows, lax.axis_index("sta") * piece % LANES, piece, 1)


def solution(mesh):
    in_specs = (
        P(("sta", "tpl"), None, None),
        P("tpl", "sta", None, None),
        P("tpl", "sta"),
        P("tpl", "sta", None),
    )
    out_specs = P("tpl", "sta")
    return jax.shard_map(
        on_device, mesh=mesh, in_specs=in_specs, out_specs=out_specs, check_vma=False
    )
```

```python
import functools

import jax
import jax.numpy as jnp
from jax import lax
from jax.experimental import pallas as pl
from jax.experimental.pallas import tpu as pltpu
from jax.sharding import PartitionSpec as P

MAXLAG = 256
WINDOW = 512
LANES = 128
SPLIT = 8
epsilon = 1e-05
MESH = pl.DeviceIdType.MESH


def round_up(value, step):
    return (value + step - 1) // step * step


def exchange_kernel(
    sizes,
    waves,
    stations,
    lags,
    records,
    got,
    gathered,
    wanted,
    send,
    keep_sems,
    send_sems,
    recv_sems,
):
    owners, sharers, padded, capacity, block_stations, stack_rows = sizes
    groups, wave_width = waves.shape
    me = lax.axis_index("sta")
    part = lax.axis_index("tpl")
    others = [lax.rem(me + step, owners) for step in range(1, owners)]
    sharing = [lax.rem(part + step, sharers) for step in range(1, sharers)]
    barrier = pltpu.get_barrier_semaphore()
    for other in others:
        pl.semaphore_signal(barrier, inc=1, device_id={"sta": other}, device_id_type=MESH)
    for other in sharing:
        pl.semaphore_signal(barrier, inc=1, device_id={"tpl": other}, device_id_type=MESH)
    own = pl.ds(pl.multiple_of(me * padded, padded), padded)

    def remote(index, source, target, device):
        return pltpu.make_async_remote_copy(
            src_ref=source,
            dst_ref=target,
            send_sem=send_sems.at[index],
            recv_sem=recv_sems.at[index],
            device_id=device,
            device_id_type=MESH,
        )

    kept = [
        pltpu.make_async_copy(send.at[own], got.at[own], keep_sems.at[0]),
        pltpu.make_async_copy(records, gathered.at[part], keep_sems.at[1]),
    ]
    kept[1].start()
    shared = [
        remote(len(others) + index, records, gathered.at[part], {"tpl": other})
        for index, other in enumerate(sharing)
    ]
    pl.semaphore_wait(barrier, len(others) + len(sharing))
    for copy in shared:
        copy.start()

    owner = stations[...] // block_stations
    block_id = lax.broadcasted_iota(jnp.int32, (groups, LANES), 1)
    member = jnp.where(owner == block_id, 1.0, 0.0)
    row = lax.broadcasted_iota(jnp.int32, (groups, groups), 0)
    earlier = row > lax.broadcasted_iota(jnp.int32, (groups, groups), 1)
    before = jnp.dot(
        jnp.where(earlier, 1.0, 0.0).astype(jnp.bfloat16),
        member.astype(jnp.bfloat16),
        preferred_element_type=jnp.float32,
    )
    rank = jnp.sum(before * member, axis=1, keepdims=True).astype(jnp.int32)
    places = lax.broadcasted_iota(jnp.int32, (groups, owners * padded), 1)
    select = jnp.where(owner * padded + rank == places, 1.0, 0.0).astype(jnp.bfloat16)
    first = owner - me // SPLIT
    block = jnp.where(first < 0, first + owners, first) + block_id
    block = jnp.where(block >= owners, block - owners, block)
    wanted[...] = block * stack_rows + block_id * capacity + rank
    detail = stations[...] - owner * block_stations
    for channel in range(3):
        detail = jnp.where(block_id == channel + 1, lags[:, channel : channel + 1], detail)
    detail = detail.astype(jnp.float32).astype(jnp.bfloat16)
    for start, rows in ((0, waves[...]), (wave_width, detail)):
        send[:, start : start + rows.shape[1]] = lax.dot_general(
            select, rows, (((0,), (0,)), ((), ())), preferred_element_type=jnp.float32
        ).astype(jnp.bfloat16)

    copies = []
    for other in others:
        rows = pl.ds(pl.multiple_of(other * padded, padded), padded)
        copies.append(remote(len(copies), send.at[rows], got.at[own], {"sta": other}))
    for copy in copies + kept[:1]:
        copy.start()
    for copy in shared + copies + kept:
        copy.wait()


def exchange(waves, stations, lags, records, sizes):
    owners, sharers, padded = sizes[:3]
    count = owners + sharers - 2
    anywhere = pl.BlockSpec(memory_space=pl.ANY)
    vmem = pl.BlockSpec(memory_space=pltpu.VMEM)
    sent = (owners * padded, waves.shape[1] + LANES)
    return pl.pallas_call(
        functools.partial(exchange_kernel, sizes),
        out_shape=(
            jax.ShapeDtypeStruct(sent, waves.dtype),
            jax.ShapeDtypeStruct((sharers,) + records.shape, records.dtype),
            jax.ShapeDtypeStruct((waves.shape[0], LANES), jnp.int32),
        ),
        in_specs=[vmem, vmem, vmem, vmem],
        out_specs=(anywhere, anywhere, vmem),
        scratch_shapes=[
            pltpu.VMEM(sent, waves.dtype),
            pltpu.SemaphoreType.DMA((2,)),
            pltpu.SemaphoreType.DMA((count,)),
            pltpu.SemaphoreType.DMA((count,)),
        ],
        compiler_params=pltpu.CompilerParams(
            collective_id=0, has_side_effects=True, vmem_limit_bytes=32 * 1024 * 1024
        ),
        name="exchange",
    )(waves, stations, lags, records)


def deliver_kernel(owners, spread, stacks, wanted, out, got, send_sems, recv_sems):
    me = lax.axis_index("sta")
    piece = WINDOW // owners
    entries = stacks.shape[0]
    others = [lax.rem(me + step, owners) for step in range(1, owners)]
    barrier = pltpu.get_barrier_semaphore()
    for other in others:
        pl.semaphore_signal(barrier, inc=1, device_id={"sta": other}, device_id_type=MESH)

    def columns(device):
        start = (device * piece) // LANES * LANES
        return pl.ds(pl.multiple_of(start, LANES), LANES)

    own = pl.ds(pl.multiple_of(me * entries, 8), entries)
    got[own, :] = stacks[:, columns(me)]
    pl.semaphore_wait(barrier, len(others))
    copies = [
        pltpu.make_async_remote_copy(
            src_ref=stacks.at[:, columns(other)],
            dst_ref=got.at[own],
            send_sem=send_sems.at[index],
            recv_sem=recv_sems.at[index],
            device_id={"sta": other},
            device_id_type=MESH,
        )
        for index, other in enumerate(others)
    ]
    for copy in copies:
        copy.start()
    places = lax.broadcasted_iota(jnp.int32, (wanted.shape[0], got.shape[0]), 1)
    marks = jnp.zeros(places.shape, jnp.float32)
    for step in range(spread):
        marks = marks + jnp.where(wanted[:, step : step + 1] == places, 1.0, 0.0)
    for copy in copies:
        copy.wait()
    out[...] = jnp.dot(
        marks, got[...], precision=lax.Precision.HIGHEST, preferred_element_type=jnp.float32
    )


def deliver(stacks, wanted, owners, spread):
    vmem = pl.BlockSpec(memory_space=pltpu.VMEM)
    return pl.pallas_call(
        functools.partial(deliver_kernel, owners, spread),
        out_shape=jax.ShapeDtypeStruct((wanted.shape[0], LANES), jnp.float32),
        in_specs=[vmem, vmem],
        out_specs=vmem,
        scratch_shapes=[
            pltpu.VMEM((owners * stacks.shape[0], LANES), jnp.float32),
            pltpu.SemaphoreType.DMA((owners - 1,)),
            pltpu.SemaphoreType.DMA((owners - 1,)),
        ],
        compiler_params=pltpu.CompilerParams(
            collective_id=1, has_side_effects=True, vmem_limit_bytes=32 * 1024 * 1024
        ),
        name="deliver",
    )(stacks, wanted)


def stack_kernel(
    sizes,
    details,
    records,
    waves,
    out,
    wide_records,
    hankel,
    scale_rows,
    wide_waves,
    wave_blocks,
    wave_scales,
):
    entries, capacity, padded, length = sizes
    channels_all, samples = wide_records.shape
    sharers = records.shape[0]
    rows_each = channels_all // sharers
    taps = length // SPLIT
    width = hankel.shape[-1]
    span = WINDOW + 2 * LANES
    parts = length // LANES
    for sharer in range(sharers):
        wide_records[rows_each * sharer : rows_each * (sharer + 1)] = records[
            sharer, :rows_each
        ].astype(jnp.float32)
    for v in range(wide_waves.shape[0]):
        wide_waves[v] = waves[:, LANES * v : LANES * (v + 1)].astype(jnp.float32)

    tap = lax.broadcasted_iota(jnp.int32, (length, SPLIT * taps), 0)
    column = lax.broadcasted_iota(jnp.int32, (length, SPLIT * taps), 1)
    spread = jnp.where(tap // SPLIT == taps - 1 - column % taps, 1.0, 0.0).astype(jnp.bfloat16)
    row_id = lax.broadcasted_iota(jnp.int32, (SPLIT * 8, length), 0)
    tap_id = lax.broadcasted_iota(jnp.int32, (SPLIT * 8, length), 1)
    own_phase = tap_id % SPLIT == SPLIT - 1 - row_id % SPLIT
    own_block = tap_id // taps == row_id // SPLIT

    def first_row(entry):
        return (entry // capacity) * (SPLIT * padded) + entry % capacity

    def prepare_waves(entry, unused):
        start = first_row(entry)
        phases = []
        for channel in range(3):
            rows = jnp.concatenate(
                [
                    wide_waves[channel * parts + v, pl.ds(start, SPLIT, stride=padded), :]
                    for v in range(parts)
                ],
                axis=1,
            )
            inverse = lax.rsqrt(
                jnp.sum(rows * rows, axis=1, keepdims=True) * (1.0 / length) + epsilon
            )
            inverse = jnp.broadcast_to(inverse[:, None, :], (SPLIT, SPLIT, LANES))
            wave_scales[entry, channel] = inverse
            rows = jnp.broadcast_to(rows[:, None, :], (SPLIT, SPLIT, length))
            rows = rows.reshape(SPLIT * SPLIT, length)
            phases.append(jnp.where(own_phase, rows, 0.0).astype(jnp.bfloat16))
        blocks = jnp.dot(
            jnp.concatenate(phases, axis=0), spread, preferred_element_type=jnp.float32
        )
        for channel in range(3):
            block = blocks[SPLIT * SPLIT * channel : SPLIT * SPLIT * (channel + 1)]
            wave_blocks[entry, channel] = jnp.where(own_block, block, 0.0).astype(jnp.bfloat16)
        return unused

    lax.fori_loop(0, entries, prepare_waves, 0, unroll=True)

    tile_rows = 32

    def prepare_scales(tile, unused):
        rows = wide_records[pl.ds(pl.multiple_of(tile * tile_rows, tile_rows), tile_rows), :]
        energy = rows * rows
        reach = 1
        while reach < length:
            energy = energy + pltpu.roll(energy, samples - reach, 1)
            reach *= 2
        inverse = lax.rsqrt(energy * (1.0 / length) + epsilon) * (1.0 / length)
        for row in range(SPLIT):
            moved = inverse if row == SPLIT - 1 else pltpu.roll(inverse, SPLIT - 1 - row, 1)
            for v in range(width // LANES):
                for eight in range(tile_rows // 8):
                    at = (tile * tile_rows + 8 * eight) * SPLIT + row
                    scale_rows[v, pl.ds(at, 8, stride=SPLIT), :] = moved[
                        8 * eight : 8 * (eight + 1), LANES * v : LANES * (v + 1)
                    ]
        return unused

    lax.fori_loop(0, channels_all // tile_rows, prepare_scales, 0)

    def prepare_hankel(channel, unused):
        row = jnp.broadcast_to(wide_records[pl.ds(channel, 1), :], (taps, samples))
        moved = pltpu.roll(
            row, samples - SPLIT * (taps - 1), 1, stride=SPLIT, stride_axis=0
        )
        hankel[channel] = moved[:, :width].astype(jnp.bfloat16)
        return unused

    lax.fori_loop(0, channels_all, prepare_hankel, 0, unroll=8)

    lane = lax.broadcasted_iota(jnp.int32, (SPLIT, LANES), 1)
    out[...] = jnp.zeros_like(out)

    def one_entry(entry):
        start = first_row(entry)
        totals = [jnp.zeros((SPLIT, LANES), jnp.float32) for _ in range(WINDOW // LANES + 1)]
        for channel in range(3):
            frames = []
            places = []
            for slot in range(SPLIT):
                base = (start + slot * padded) * 4
                place = details[base] * 3 + channel
                lag = details[base + 1 + channel]
                left = pl.multiple_of((lag // LANES) * LANES, LANES)
                places.append((place, lag % LANES, lag // LANES))
                frames.append(hankel[place, :, pl.ds(left, span)])
            terms = jnp.dot(
                wave_blocks[entry, channel],
                jnp.concatenate(frames, axis=0),
                preferred_element_type=jnp.float32,
            )
            for slot in range(SPLIT):
                place, rest, left = places[slot]
                shift = (LANES - rest) % LANES
                scale_at = pl.ds(pl.multiple_of(place * SPLIT, SPLIT), SPLIT)
                inverse = wave_scales[entry, channel, slot]
                moved = []
                for v in range(span // LANES):
                    part = terms[SPLIT * slot : SPLIT * (slot + 1), LANES * v : LANES * (v + 1)]
                    normed = part * (scale_rows[left + v, scale_at, :] * inverse)
                    moved.append(pltpu.roll(normed, shift, 1))
                carried = lane >= LANES - rest
                for v in range(len(totals)):
                    totals[v] = totals[v] + jnp.where(carried, moved[v + 1], moved[v])
        whole = jnp.concatenate(totals, axis=1)
        whole = pltpu.roll(
            whole, whole.shape[1] - (SPLIT - 1), 1, stride=1, stride_axis=0
        )
        out[pl.ds(entry, 1), :] = jnp.sum(whole[:, :WINDOW], axis=0, keepdims=True)

    def some_entries(turn, unused):
        for step in range(2):
            one_entry(jnp.minimum(turn * 2 + step, entries - 1))
        return unused

    lax.fori_loop(0, (entries + 1) // 2, some_entries, 0)


def stack_entries(details, records, waves, rows_each, length, entries, capacity, padded):
    sharers, _, samples = records.shape
    channels_all = sharers * rows_each
    width = WINDOW + MAXLAG + LANES
    vmem = pl.BlockSpec(memory_space=pltpu.VMEM)
    return pl.pallas_call(
        functools.partial(stack_kernel, (entries, capacity, padded, length)),
        out_shape=jax.ShapeDtypeStruct((round_up(entries, 8), WINDOW), jnp.float32),
        in_specs=[pl.BlockSpec(memory_space=pltpu.SMEM), vmem, vmem],
        out_specs=vmem,
        scratch_shapes=[
            pltpu.VMEM((channels_all, samples), jnp.float32),
            pltpu.VMEM((channels_all, length // SPLIT, width), jnp.bfloat16),
            pltpu.VMEM((width // LANES, channels_all * SPLIT, LANES), jnp.float32),
            pltpu.VMEM((3 * length // LANES, waves.shape[0], LANES), jnp.float32),
            pltpu.VMEM((entries, 3, SPLIT * SPLIT, length), jnp.bfloat16),
            pltpu.VMEM((entries, 3, SPLIT, SPLIT, LANES), jnp.float32),
        ],
        compiler_params=pltpu.CompilerParams(vmem_limit_bytes=40 * 1024 * 1024),
        name="stack_entries",
    )(details, records, waves)


def on_device(records, waveforms, station_ids, lag_steps):
    owners = lax.axis_size("sta")
    sharers = lax.axis_size("tpl")
    groups = waveforms.shape[0]
    length = waveforms.shape[-1]
    block_stations = records.shape[0] * sharers
    spread = owners // SPLIT
    capacity = (groups + owners - 1) // owners + 1
    padded = round_up(capacity, 16)
    rows_each = records.shape[0] * 3
    flat_records = records.reshape(rows_each, records.shape[-1])
    flat_records = jnp.pad(flat_records, ((0, round_up(rows_each, 16) - rows_each), (0, 0)))
    entries = spread * capacity
    stack_rows = round_up(entries, 8)
    got, gathered, wanted = exchange(
        waveforms.reshape(groups, 3 * length),
        station_ids,
        lag_steps[:, 0, :],
        flat_records,
        (owners, sharers, padded, capacity, block_stations, stack_rows),
    )
    got_details = got[:, 3 * length : 3 * length + 4].astype(jnp.int32).reshape(-1)
    stacks = stack_entries(
        got_details, gathered, got, rows_each, length, entries, capacity, padded
    )
    rows = deliver(stacks, wanted, owners, spread)
    piece = WINDOW // owners
    return lax.dynamic_slice_in_dim(rows, lax.axis_index("sta") * piece % LANES, piece, 1)


def solution(mesh):
    in_specs = (
        P(("sta", "tpl"), None, None),
        P("tpl", "sta", None, None),
        P("tpl", "sta"),
        P("tpl", "sta", None),
    )
    out_specs = P("tpl", "sta")
    return jax.shard_map(
        on_device, mesh=mesh, in_specs=in_specs, out_specs=out_specs, check_vma=False
    )
```
